512 devices in a mesh: slab: 32 (over z_hi, y, x), patch: 16 (over z_lo, core).
Axes of the slice: x: 4, y: 4, z: 16 (z_hi: 2, z_lo: 8; z = z_hi * 8 + z_lo), core: 2. Of those that a mesh axis runs over, the one named last changes fastest.
Arguments:
- rhs: float32 [32, 16, 128, 2, 256], P('slab', 'patch'), may hold values from -12 to 12
- face_blocks: bfloat16 [32, 16, 4, 256, 256], P('slab', 'patch'), may hold values from -1 to 4, as said below
- interior_inverse: bfloat16 [32, 16, 1024, 1024], P('slab', 'patch'), may hold values from -1 to 1, as said below
- coarse_inverse: bfloat16 [8192, 8192], P('slab', 'patch'), may hold values from -1 to 3, as said below
- primal_ids: int32 [32, 16, 16], P('slab', 'patch'), may hold values from 0 to 1023, as said below
Outputs:
- solution: float32 [32, 16, 128, 2, 256], P('slab', 'patch')
- residual: float32 [32, 16, 128, 2, 256], P('slab', 'patch')
The draws below stay inside these ranges and needn't reach their ends.
Inputs may be any that keep to these rules, and one draw needn't show every extreme that they name: `face_blocks`: each block is symmetric positive definite. `interior_inverse`: each patch's matrix is symmetric. `coarse_inverse`: the matrix, read with columns in mesh order of patches, is symmetric positive definite. `primal_ids`: each patch's 16 entries are distinct.
All inputs are finite; a program needn't handle non-finite values.
Results may differ from the reference program's by a relative error of at most 0.0095.
The reference program's roundings to bfloat16 on the way count: a program that leaves them out, or rounds other values in their place, can miss the bound.
Values may be sent and summed in bfloat16 or wider, within the bound.
No kernel may reach another device: no remote copies, remote signals or barrier semaphores. Data moves between devices by JAX's collectives and lax.ppermute only.
A program may use at most 64 MiB of HBM per device.

```python
import math
import jax
import jax.numpy as jnp
from jax import lax

F = 256
NI = 1024
PRIM = 16
RHS = 128
ITERS = 2
COARSE = 8192
N_SLAB = 32
N_PATCH = 16


def symmetric_block(key, order, radius, lowest, highest):
    key_off, key_diag = jax.random.split(key)
    noise = jax.random.uniform(key_off, (order, order), jnp.float32, -1.0, 1.0)
    factor = radius / (2.0 * math.sqrt(2.0 * order / 3.0))
    diag_values = jax.random.uniform(key_diag, (order,), jnp.float32, lowest, highest)
    return (noise + noise.T) * factor + jnp.diag(diag_values)


def draw_face_blocks(key, part):
    key = jax.random.fold_in(key, 11)

    def one_block(number):
        return symmetric_block(jax.random.fold_in(key, number), F, 0.5, 1.5, 3.0).astype(jnp.bfloat16)
    return lax.map(one_block, jnp.arange(N_SLAB * N_PATCH * 4)).reshape(N_SLAB, N_PATCH, 4, F, F)


def draw_interior_inverse(key, part):
    key = jax.random.fold_in(key, 12)

    def one_block(number):
        return symmetric_block(jax.random.fold_in(key, number), NI, 0.2, 0.2, 0.6).astype(jnp.bfloat16)
    return lax.map(one_block, jnp.arange(N_SLAB * N_PATCH)).reshape(N_SLAB, N_PATCH, NI, NI)


def draw_coarse_inverse(key, part):
    key = jax.random.fold_in(key, 13)
    whole = symmetric_block(key, COARSE, 0.3, 0.5, 2.0)
    whole = whole.reshape(COARSE, N_SLAB, N_PATCH, PRIM).transpose(0, 2, 1, 3).reshape(COARSE, COARSE)
    return whole.astype(jnp.bfloat16)


def draw_primal_ids(key, part):
    key = jax.random.fold_in(key, 14)
    patch_keys = jax.random.split(key, N_SLAB * N_PATCH)

    def one_patch(patch_key):
        return jax.random.permutation(patch_key, NI)[:PRIM]
    return jax.vmap(one_patch)(patch_keys).astype(jnp.int32).reshape(N_SLAB, N_PATCH, PRIM)


def block_levels(rng, shape, pieces, low, top_value):
    gain, own = 1.0, jax.random.fold_in(rng, 6)
    for dim, blocks in pieces:
        steps = jnp.exp(jax.random.uniform(jax.random.fold_in(own, dim), (blocks,), jnp.float32, low / len(pieces), top_value / len(pieces)))
        gain = gain * jnp.repeat(steps, shape[dim] // blocks).reshape([-1 if axis == dim else 1 for axis in range(len(shape))])
    return gain


def scatter_about(rng, dims, scale, most, pieces=(), kind=jnp.bfloat16):
    array = jax.random.normal(rng, dims, jnp.float32) * scale
    if len(pieces) > 0:
        array = block_levels(rng, dims, pieces, -0.22, 0.18) * array
    return jnp.clip(array, min=-most, max=most).astype(kind)


def setup_inputs(seed: int = 0) -> dict:
    splits = jax.random.split(jax.random.key(seed), 6)
    return {
        "rhs": scatter_about(splits[0], (N_SLAB, N_PATCH, RHS, 2, F), 2.0, 12.0, ((0, 32), (1, 16)), jnp.float32),
        "face_blocks": draw_face_blocks(jax.random.fold_in(splits[5], 71), 0),
        "interior_inverse": draw_interior_inverse(jax.random.fold_in(splits[5], 71), 0),
        "coarse_inverse": draw_coarse_inverse(jax.random.fold_in(splits[5], 71), 0),
        "primal_ids": draw_primal_ids(jax.random.fold_in(splits[5], 71), 0),
    }


def face_solve(factors, vector):
    moved = jnp.moveaxis(vector, -3, -1)
    middle = jax.scipy.linalg.solve_triangular(factors, moved, lower=True)
    result = jax.scipy.linalg.solve_triangular(factors, middle, lower=True, trans=1)
    return jnp.moveaxis(result, -1, -3)

def face_apply(blocks, vb):
    return jnp.einsum('fij,rfj->rfi', blocks.astype(jnp.float32), vb.astype(jnp.float32), precision=lax.Precision.HIGHEST)

def interior_apply(inverse, vb):
    flat = vb.reshape(vb.shape[0], -1)
    return jnp.dot(flat.astype(jnp.float32), inverse.T.astype(jnp.float32), preferred_element_type=jnp.float32).reshape(vb.shape)

def patch_view(owned_field):
    return jnp.stack([owned_field[:, :, :, 0], owned_field[:, :, :, 1], jnp.roll(owned_field[:, :, :, 0], 1, 0), jnp.roll(owned_field[:, :, :, 1], 1, 1)], axis=3)

def assemble(patch_terms):
    return jnp.stack([patch_terms[:, :, :, 0] + jnp.roll(patch_terms[:, :, :, 2], -1, 0), patch_terms[:, :, :, 1] + jnp.roll(patch_terms[:, :, :, 3], -1, 1)], axis=3)

def inner_total(first, second):
    return jnp.sum(first * second, axis=(0, 1, 3, 4))

def reference(rhs, face_blocks, interior_inverse, coarse_inverse, primal_ids):
    count = N_SLAB * N_PATCH
    sum_slab = face_blocks[:, :, 0].astype(jnp.float32) + jnp.roll(face_blocks[:, :, 2], -1, 0).astype(jnp.float32)
    sum_patch = face_blocks[:, :, 1].astype(jnp.float32) + jnp.roll(face_blocks[:, :, 3], -1, 1).astype(jnp.float32)
    factors = jnp.linalg.cholesky(jnp.stack([sum_slab, sum_patch], axis=2))
    blocks_flat = face_blocks.reshape(count, 4, F, F)
    inverse_flat = interior_inverse.reshape(count, NI, NI)
    ids_flat = primal_ids.reshape(count, PRIM)

    def local_operator(patch_parts):
        blocks, inverse, vb = patch_parts
        return face_apply(blocks, vb) - interior_apply(inverse, vb)

    def apply_s(vector):
        vb = patch_view(vector).astype(jnp.bfloat16).reshape(count, RHS, 4, F)
        terms = lax.map(local_operator, (blocks_flat, inverse_flat, vb))
        return assemble(terms.reshape(N_SLAB, N_PATCH, RHS, 4, F))

    def primal_part(patch_parts):
        blocks, indices, vb = patch_parts
        product = face_apply(blocks, vb).reshape(RHS, NI)
        return jnp.take(product, indices, axis=1).T.astype(jnp.bfloat16)

    def extend(patch_parts):
        blocks, inverse, indices, vb, coarse_sol = patch_parts
        spread = jnp.zeros((RHS, NI), jnp.float32).at[:, indices].set(coarse_sol.T.astype(jnp.float32))
        spread = spread.astype(jnp.bfloat16).reshape(RHS, 4, F)
        return interior_apply(inverse, vb) + face_apply(blocks, spread)

    def apply_m(vector):
        lifted = face_solve(factors, vector)
        hb = patch_view(lifted).astype(jnp.bfloat16).reshape(count, RHS, 4, F)
        coarse_rhs = lax.map(primal_part, (blocks_flat, ids_flat, hb))
        ordered = coarse_rhs.reshape(N_SLAB, N_PATCH, PRIM, RHS).transpose(1, 0, 2, 3).reshape(COARSE, RHS)
        coarse_sol = jnp.dot(coarse_inverse.astype(jnp.float32), ordered.astype(jnp.float32), preferred_element_type=jnp.float32).astype(jnp.bfloat16)
        coarse_sol = coarse_sol.reshape(count, PRIM, RHS)
        terms = lax.map(extend, (blocks_flat, inverse_flat, ids_flat, hb, coarse_sol))
        return lifted + face_solve(factors, assemble(terms.reshape(N_SLAB, N_PATCH, RHS, 4, F)))
    solution = jnp.zeros_like(rhs)
    residual = rhs
    direction = apply_m(residual)
    rz_now = inner_total(residual, direction)
    for iteration in range(ITERS):
        mapped = apply_s(direction)
        step_size = rz_now / inner_total(direction, mapped)
        solution = solution + step_size[:, None, None] * direction
        residual = residual - step_size[:, None, None] * mapped
        if iteration + 1 < ITERS:
            precond = apply_m(residual)
            rz_next = inner_total(residual, precond)
            direction = precond + (rz_next / rz_now)[:, None, None] * direction
            rz_now = rz_next
    return (solution, residual)
```

```python
import jax
import jax.numpy as jnp
from jax import lax
from jax.experimental import pallas as pl
from jax.experimental.pallas import tpu as pltpu
from jax.sharding import Mesh, PartitionSpec as P

F = 256
NI = 1024
RHS = 128
PRIM = 16
OWN = 2 * F
SLAB = ("zh", "y", "x")
PATCH = ("zl", "core")
COLUMN = ("zh", "zl", "core")
PLANE = ("y", "x")
HIGHEST = lax.Precision.HIGHEST
ROUGH_STEPS = 12
FINE_STEPS = 64
VMEM = pl.BlockSpec(memory_space=pltpu.VMEM)
SMEM = pl.BlockSpec(memory_space=pltpu.SMEM)


def odd_pairs(count):
    return [(i, i ^ 1) for i in range(count)]


def even_pairs(count):
    return [(i, (i + 1) % count if i % 2 else (i - 1) % count) for i in range(count)]


def roll_pairs(count, by):
    return [(i, (i + by) % count) for i in range(count)]


def call(kernel, out_shapes, in_specs, name, flops=0, scratch=()):
    return pl.pallas_call(
        kernel,
        out_shape=out_shapes,
        in_specs=in_specs,
        out_specs=jax.tree.map(lambda _: VMEM, out_shapes),
        scratch_shapes=list(scratch),
        compiler_params=pltpu.CompilerParams(vmem_limit_bytes=16 * 1024 * 1024),
        cost_estimate=pl.CostEstimate(flops=flops, bytes_accessed=1 << 20, transcendentals=0),
        name=name,
    )


def f32(*shape):
    return jax.ShapeDtypeStruct(shape, jnp.float32)


def bf16(*shape):
    return jax.ShapeDtypeStruct(shape, jnp.bfloat16)


def fine_dot(a, b):
    return jnp.dot(a, b, precision=HIGHEST, preferred_element_type=jnp.float32)


def rough_dot(a, b):
    return jnp.dot(a, b, preferred_element_type=jnp.float32)


def rows(number):
    return slice(number * F, (number + 1) * F)


def prepare_kernel(even_ref, rhs_ref, blocks_ref, slab_b, first_ref, patch_b, slab_a, patch_a, second_ref):
    for even, ahead, back, a_ref, b_ref in ((even_ref[0], 0, 2, slab_a, slab_b), (even_ref[1], 1, 3, patch_a, patch_b)):
        @pl.when(even == 1)
        def _():
            b_ref[...] = blocks_ref[back]
            a_ref[...] = blocks_ref[ahead]

        @pl.when(even == 0)
        def _():
            b_ref[...] = blocks_ref[ahead]
            a_ref[...] = blocks_ref[back]

    first_ref[...] = rhs_ref[:, 0, :].T
    second_ref[...] = rhs_ref[:, 1, :].T


def primal_kernel(ids_ref, blocks_ref, primal_ref):
    row = lax.broadcasted_iota(jnp.int32, (PRIM, NI), 0)
    picked = jnp.zeros((PRIM, NI), jnp.int32)
    for k in range(PRIM):
        picked = jnp.where(row == k, ids_ref[k], picked)
    onehot = (picked == lax.broadcasted_iota(jnp.int32, (PRIM, NI), 1)).astype(jnp.float32).astype(jnp.bfloat16)
    for f in range(4):
        primal_ref[:, rows(f)] = rough_dot(onehot[:, rows(f)], blocks_ref[f]).astype(jnp.bfloat16)


def invert_kernel(even_ref, blocks_ref, slab_b, patch_b, slab_a, patch_a, out_ref, a_ref):
    index = lax.broadcasted_iota(jnp.int32, (F, F), 0)
    unit = (index == lax.broadcasted_iota(jnp.int32, (F, F), 1)).astype(jnp.float32)

    def start(f):
        bound = jnp.max(jnp.sum(jnp.abs(a_ref[f]), axis=0, keepdims=True), axis=1, keepdims=True)
        return unit * (1.9 / bound)

    for f in range(4):
        b, a = ((slab_b, slab_a), (patch_b, patch_a))[f % 2]
        other = jnp.where(even_ref[f % 2] == (1 if f < 2 else 0), a[...], b[...])
        a_ref[f] = blocks_ref[f].astype(jnp.float32) + other.astype(jnp.float32)
        out_ref[f] = start(f)

    def newton(multiply):
        lefts = [unit - multiply(a_ref[f], out_ref[f]) for f in range(4)]
        worst = jnp.float32(0.0)
        for f in range(4):
            worst = jnp.maximum(worst, jnp.sum(lefts[f] * lefts[f]))
        for f in range(4):
            out_ref[f] = out_ref[f] + multiply(out_ref[f], lefts[f])
        return worst

    def rough(a, b):
        return rough_dot(a.astype(jnp.bfloat16), b.astype(jnp.bfloat16))

    def rough_body(carry):
        step, _ = carry
        return step + 1, newton(rough)

    _, worst = lax.while_loop(lambda c: (c[0] < ROUGH_STEPS) & ~(c[1] < 0.25), rough_body, (0, jnp.float32(1e30)))

    @pl.when(~(worst < 0.25))
    def _():
        for f in range(4):
            out_ref[f] = start(f)

    def fine_body(carry):
        step, last, _ = carry
        return step + 1, newton(fine_dot), last

    lax.while_loop(
        lambda c: (c[0] < FINE_STEPS) & (c[1] > 1e-6) & ~((c[1] < 1e-2) & (c[1] >= c[2])),
        fine_body, (0, jnp.float32(1e30), jnp.float32(1e31)))


def solve_and_restrict(residual_of, factors_ref, primal_ref, lifted_ref, rounded_ref, c_ref):
    for f in range(4):
        lifted = fine_dot(factors_ref[f], residual_of(f))
        lifted_ref[rows(f)] = lifted
        rounded_ref[rows(f)] = lifted.astype(jnp.bfloat16)
    c = rough_dot(primal_ref[...], rounded_ref[...]).astype(jnp.bfloat16)
    for j in range(32):
        c_ref[j] = c


def first_kernel(own_ref, second_ref, slab_ref, patch_ref, factors_ref, primal_ref, residual_ref, lifted_ref, rounded_ref, c_ref):
    residual_ref[rows(0)] = own_ref[...]
    residual_ref[rows(1)] = second_ref[...]
    residual_ref[rows(2)] = slab_ref[...]
    residual_ref[rows(3)] = patch_ref[...]
    solve_and_restrict(lambda f: residual_ref[rows(f)], factors_ref, primal_ref, lifted_ref, rounded_ref, c_ref)


def write_parts(even_ref, terms_ref, outs):
    slab_b, patch_b, slab_a, patch_a = outs
    for even, ahead, back, a_ref, b_ref in ((even_ref[0], 0, 2, slab_a, slab_b), (even_ref[1], 1, 3, patch_a, patch_b)):
        upper, lower = terms_ref[rows(ahead)], terms_ref[rows(back)]
        b_ref[...] = jnp.where(even == 1, lower, upper)
        a_ref[...] = jnp.where(even == 1, upper, lower)


def assembled(even_ref, terms_ref, got, f):
    slab_b, patch_b, slab_a, patch_a = got
    a_ref, b_ref = ((slab_a, slab_b), (patch_a, patch_b))[f % 2]
    use_a = even_ref[f % 2] == (1 if f < 2 else 0)
    return terms_ref[rows(f)] + jnp.where(use_a, a_ref[...], b_ref[...])


def coarse_kernel(coarse_ref, gathered_ref, out_ref):
    gathered = gathered_ref[...].reshape(OWN, RHS)
    out_ref[...] = rough_dot(coarse_ref[...], gathered).reshape(16, PRIM, RHS)


def repeat_rows(out_ref, value):
    for j in range(out_ref.shape[0]):
        out_ref[j] = value


def sum_kernel(parts_ref, out_ref):
    repeat_rows(out_ref, jnp.sum(parts_ref[...], axis=0))


def terms_kernel(even_ref, parts_ref, inverse_ref, rounded_ref, primal_ref, residual_ref, lifted_ref, terms_ref,
                 product_ref, *outs):
    u = jnp.sum(parts_ref[...], axis=0).astype(jnp.bfloat16)
    product = jnp.zeros((1, RHS), jnp.float32)
    for f in range(4):
        term = rough_dot(inverse_ref[rows(f)], rounded_ref[...]) + lax.dot_general(
            primal_ref[:, rows(f)], u, (((0,), (0,)), ((), ())), preferred_element_type=jnp.float32)
        terms_ref[rows(f)] = term
        lifted = lifted_ref[rows(f)]
        weight = term + residual_ref[rows(f)] if f < 2 else term
        product = product + jnp.sum(lifted * weight, axis=0, keepdims=True)
    repeat_rows(product_ref, product)
    write_parts(even_ref, terms_ref, outs)


def direction_kernel(again, *refs):
    if again:
        sums_ref, before_ref, last_ref, *refs = refs
        scale = jnp.sum(sums_ref[...], axis=0) / jnp.sum(before_ref[...], axis=0)[:1]
    else:
        over_ref, *refs = refs
    (even_ref, terms_ref, slab_b, patch_b, slab_a, patch_a, lifted_ref, factors_ref, blocks_ref, inverse_ref,
     direction_ref, image_ref, product_ref, *outs, rounded_ref) = refs
    got = (slab_b, patch_b, slab_a, patch_a)
    for f in range(4):
        value = lifted_ref[rows(f)] + fine_dot(factors_ref[f], assembled(even_ref, terms_ref, got, f))
        if again:
            value = value + scale * last_ref[rows(f)]
        direction_ref[rows(f)] = value
        rounded_ref[rows(f)] = value.astype(jnp.bfloat16)
    product = jnp.zeros((1, RHS), jnp.float32)
    for f in range(4):
        image = rough_dot(blocks_ref[f], rounded_ref[rows(f)]) - rough_dot(inverse_ref[rows(f)], rounded_ref[...])
        image_ref[rows(f)] = image
        product = product + jnp.sum(direction_ref[rows(f)] * image, axis=0, keepdims=True)
    repeat_rows(product_ref, product if again else jnp.concatenate([over_ref[0], product], axis=0))
    if again:
        outs[0][...] = image_ref[rows(2)]
        outs[1][...] = image_ref[rows(3)]
    else:
        write_parts(even_ref, image_ref, outs)


def update_kernel(even_ref, sums_ref, image_ref, slab_b, patch_b, slab_a, patch_a, last_ref, factors_ref, primal_ref,
                  residual_ref, lifted_ref, rounded_ref, c_ref):
    sums = jnp.sum(sums_ref[...], axis=0)
    step = sums[:1] / sums[1:]
    got = (slab_b, patch_b, slab_a, patch_a)
    for f in range(4):
        residual_ref[rows(f)] = last_ref[rows(f)] - step * assembled(even_ref, image_ref, got, f)
    solve_and_restrict(lambda f: residual_ref[rows(f)], factors_ref, primal_ref, lifted_ref, rounded_ref, c_ref)


def last_kernel(first_ref, over_ref, under_ref, first_direction_ref, direction_ref, residual_ref, image_ref,
                slab_ref, patch_ref, solution_ref, out_ref):
    first = jnp.sum(first_ref[...], axis=0)
    first_step = first[:1] / first[1:]
    step = jnp.sum(over_ref[...], axis=0) / jnp.sum(under_ref[...], axis=0)
    for f, got in ((0, slab_ref), (1, patch_ref)):
        value = first_step * first_direction_ref[rows(f)] + step * direction_ref[rows(f)]
        left = residual_ref[rows(f)] - step * (image_ref[rows(f)] + got[...])
        solution_ref[:, f, :] = value.T
        out_ref[:, f, :] = left.T


def swap(parts):
    slab_b, patch_b, slab_a, patch_a = parts
    return (
        lax.ppermute(slab_b, SLAB, even_pairs(32)),
        lax.ppermute(patch_b, PATCH, even_pairs(16)),
        lax.ppermute(slab_a, SLAB, odd_pairs(32)),
        lax.ppermute(patch_a, PATCH, odd_pairs(16)),
    )


def total_parts(spread):
    parts = lax.all_to_all(spread, COLUMN, 0, 0)
    spread = call(sum_kernel, f32(16, *spread.shape[1:]), [VMEM], "sum")(parts)
    return lax.all_to_all(spread, PLANE, 0, 0)


def on_device(rhs, face_blocks, interior_inverse, coarse_inverse, primal_ids):
    blocks = face_blocks[0, 0]
    inverse = interior_inverse[0, 0]
    ids = primal_ids[0, 0]
    slab_even = 1 - lax.axis_index("x") % 2
    patch_even = 1 - lax.axis_index("core")
    even = jnp.stack([slab_even, patch_even]).astype(jnp.int32)

    slab_b, first, patch_b, slab_a, patch_a, second = call(
        prepare_kernel, [bf16(F, F), f32(F, RHS)] + [bf16(F, F)] * 3 + [f32(F, RHS)], [SMEM, VMEM, VMEM], "prepare")(
            even, rhs[0, 0], blocks)
    slab_b = lax.ppermute(slab_b, SLAB, even_pairs(32))
    from_slab = lax.ppermute(first, SLAB, roll_pairs(32, 1))
    patch_b = lax.ppermute(patch_b, PATCH, even_pairs(16))
    slab_a = lax.ppermute(slab_a, SLAB, odd_pairs(32))
    patch_a = lax.ppermute(patch_a, PATCH, odd_pairs(16))
    from_patch = lax.ppermute(second, PATCH, roll_pairs(16, 1))
    primal = call(primal_kernel, bf16(PRIM, NI), [SMEM, VMEM], "primal")(ids, blocks)
    slab_b, from_slab, patch_b, slab_a, patch_a, from_patch = lax.optimization_barrier(
        (slab_b, from_slab, patch_b, slab_a, patch_a, from_patch))
    got = (slab_b, patch_b, slab_a, patch_a)

    factors = call(invert_kernel, f32(4, F, F), [SMEM] + [VMEM] * 5, "invert", 4 * 16 * 2 * F ** 3,
                   [pltpu.VMEM((4, F, F), jnp.float32)])(even, blocks, *got)

    field = f32(NI, RHS)
    part = [f32(F, RHS)] * 4
    solved = [field, field, bf16(NI, RHS), bf16(32, PRIM, RHS)]
    solve_flops = 4 * 12 * F * F * RHS

    def coarse_terms(residual, lifted, rounded, c):
        gathered = lax.all_to_all(c, SLAB, 0, 0)
        partial = call(coarse_kernel, f32(16, PRIM, RHS), [VMEM] * 2, "coarse", 1 << 25)(coarse_inverse, gathered)
        parts = lax.all_to_all(partial, PATCH, 0, 0)
        terms, product, *send = call(
            terms_kernel, [field, f32(32, 1, RHS)] + part, [SMEM] + [VMEM] * 6, "terms", 1 << 28)(
                even, parts, inverse, rounded, primal, residual, lifted)
        return terms, product, send

    scratch = [pltpu.VMEM((NI, RHS), jnp.bfloat16)]
    residual, lifted, rounded, c = call(first_kernel, solved, [VMEM] * 6, "first", solve_flops)(
        first, second, from_slab, from_patch, factors, primal)
    terms, product, send = coarse_terms(residual, lifted, rounded, c)
    got = swap(send)
    first_direction, image, spread, *send = call(
        lambda *refs: direction_kernel(False, *refs), [field, field, f32(32, 2, RHS)] + part,
        [VMEM, SMEM] + [VMEM] * 9, "direction", solve_flops, scratch)(
            product, even, terms, *got, lifted, factors, blocks, inverse)

    got = swap(send)
    first_sums = total_parts(spread)
    first_sums, got = lax.optimization_barrier((first_sums, got))
    residual, lifted, rounded, c = call(update_kernel, solved, [SMEM] + [VMEM] * 9, "update", solve_flops)(
        even, first_sums, image, *got, residual, factors, primal)
    terms, spread, send = coarse_terms(residual, lifted, rounded, c)
    got = swap(send)
    over = total_parts(spread)
    over, got = lax.optimization_barrier((over, got))
    direction, image, spread, *send = call(
        lambda *refs: direction_kernel(True, *refs), [field, field, f32(32, 1, RHS)] + part[:2],
        [VMEM] * 3 + [SMEM] + [VMEM] * 9, "direction_again", solve_flops, scratch)(
            over, first_sums, first_direction, even, terms, *got, lifted, factors, blocks, inverse)

    from_slab = lax.ppermute(send[0], SLAB, roll_pairs(32, -1))
    from_patch = lax.ppermute(send[1], PATCH, roll_pairs(16, -1))
    under = total_parts(spread)
    under, from_slab, from_patch = lax.optimization_barrier((under, from_slab, from_patch))
    solution, residual = call(last_kernel, [f32(RHS, 2, F)] * 2, [VMEM] * 9, "last")(
        first_sums, over, under, first_direction, direction, residual, image, from_slab, from_patch)
    return (solution.reshape(1, 1, RHS, 2, F), residual.reshape(1, 1, RHS, 2, F))


def solution(mesh):
    chips = Mesh(mesh.devices.reshape(2, 4, 4, 8, 2), ("zh", "y", "x", "zl", "core"))
    return jax.shard_map(
        on_device,
        mesh=chips,
        in_specs=(
            P(SLAB, PATCH, None, None, None),
            P(SLAB, PATCH, None, None, None),
            P(SLAB, PATCH, None, None),
            P(SLAB, PATCH),
            P(SLAB, PATCH, None),
        ),
        out_specs=(P(SLAB, PATCH, None, None, None), P(SLAB, PATCH, None, None, None)),
        check_vma=False,
    )
```

```python
import jax
import jax.numpy as jnp
from jax import lax
from jax.experimental import pallas as pl
from jax.experimental.pallas import tpu as pltpu
from jax.sharding import Mesh, PartitionSpec as P

F = 256
NI = 1024
RHS = 128
PRIM = 16
OWN = 2 * F
SLAB = ("zh", "y", "x")
PATCH = ("zl", "core")
COLUMN = ("zh", "zl", "core")
PLANE = ("y", "x")
HIGHEST = lax.Precision.HIGHEST
ROUGH_STEPS = 6
FINE_STEPS = 32
VMEM = pl.BlockSpec(memory_space=pltpu.VMEM)
SMEM = pl.BlockSpec(memory_space=pltpu.SMEM)


def odd_pairs(count):
    return [(i, i ^ 1) for i in range(count)]


def even_pairs(count):
    return [(i, (i + 1) % count if i % 2 else (i - 1) % count) for i in range(count)]


def roll_pairs(count, by):
    return [(i, (i + by) % count) for i in range(count)]


def call(kernel, out_shapes, in_specs, name, flops=0, scratch=()):
    return pl.pallas_call(
        kernel,
        out_shape=out_shapes,
        in_specs=in_specs,
        out_specs=jax.tree.map(lambda _: VMEM, out_shapes),
        scratch_shapes=list(scratch),
        compiler_params=pltpu.CompilerParams(vmem_limit_bytes=16 * 1024 * 1024),
        cost_estimate=pl.CostEstimate(flops=flops, bytes_accessed=1 << 20, transcendentals=0),
        name=name,
    )


def f32(*shape):
    return jax.ShapeDtypeStruct(shape, jnp.float32)


def bf16(*shape):
    return jax.ShapeDtypeStruct(shape, jnp.bfloat16)


def fine_dot(a, b):
    return jnp.dot(a, b, precision=HIGHEST, preferred_element_type=jnp.float32)


def rough_dot(a, b):
    return jnp.dot(a, b, preferred_element_type=jnp.float32)


def rows(number):
    return slice(number * F, (number + 1) * F)


HALF = F // 2
PAD = 16
PACKED = F + PAD


def square_masks():
    row = lax.broadcasted_iota(jnp.int32, (HALF, HALF), 0)
    column = lax.broadcasted_iota(jnp.int32, (HALF, HALF), 1)
    return row > column, row == column, row < column


def turn_kernel(rhs_ref, first_ref, second_ref):
    first_ref[...] = rhs_ref[:, 0, :].T
    second_ref[...] = rhs_ref[:, 1, :].T


def pack_kernel(even_ref, second_ref, blocks_ref, slab_b, patch_b, slab_a, patch_a):
    lower, diagonal, upper = square_masks()
    for f in range(4):
        b_ref, a_ref = ((slab_b, slab_a), (patch_b, patch_a))[f % 2]
        use_a = even_ref[f % 2] == (1 if f < 2 else 0)

        def pack(out_ref):
            kind = out_ref.dtype
            block = blocks_ref[f].astype(jnp.float32)
            first, second = block[:HALF, :HALF], block[HALF:, HALF:]
            out_ref[:HALF] = jnp.where(upper, second, first).astype(kind)
            out_ref[HALF:F] = block[HALF:, :HALF].astype(kind)
            row = jnp.sum(jnp.where(diagonal, second, 0.0), axis=0, keepdims=True)
            out_ref[F:PACKED] = jnp.broadcast_to(row, (PAD, HALF)).astype(kind)
            if f % 2:
                out_ref[PACKED:] = second_ref[...]

        @pl.when(use_a)
        def _():
            pack(a_ref)

        @pl.when(jnp.logical_not(use_a))
        def _():
            pack(b_ref)


def unpack(part_ref, out_ref):
    lower, diagonal, upper = square_masks()
    mixed, below = part_ref[:HALF].astype(jnp.float32), part_ref[HALF:F].astype(jnp.float32)
    corner = part_ref[F:PACKED].astype(jnp.float32)[:1]
    first = jnp.where(upper, 0.0, mixed)
    second = jnp.where(upper, mixed, 0.0)
    out_ref[:HALF, :HALF] = out_ref[:HALF, :HALF] + (first + jnp.where(lower, first, 0.0).T)
    out_ref[HALF:, HALF:] = out_ref[HALF:, HALF:] + (
        second + second.T + jnp.where(diagonal, corner, 0.0))
    out_ref[HALF:, :HALF] = out_ref[HALF:, :HALF] + below
    out_ref[:HALF, HALF:] = out_ref[:HALF, HALF:] + below.T


def primal_kernel(ids_ref, blocks_ref, primal_ref):
    row = lax.broadcasted_iota(jnp.int32, (PRIM, NI), 0)
    picked = jnp.zeros((PRIM, NI), jnp.int32)
    for k in range(PRIM):
        picked = jnp.where(row == k, ids_ref[k], picked)
    onehot = (picked == lax.broadcasted_iota(jnp.int32, (PRIM, NI), 1)).astype(jnp.float32).astype(jnp.bfloat16)
    for f in range(4):
        primal_ref[:, rows(f)] = rough_dot(onehot[:, rows(f)], blocks_ref[f]).astype(jnp.bfloat16)


def invert_kernel(flag, even_ref, part_b, part_a, blocks_ref, right_ref, shared_ref, factors_ref, residual_ref,
                  lifted_ref, a_ref):
    for k in range(2):
        use_a = even_ref[flag] == 1 - k
        a_ref[k] = blocks_ref[2 * k + flag].astype(jnp.float32)

        def take(part_ref):
            unpack(part_ref, a_ref.at[k])
            if k == 1 and flag == 1:
                residual_ref[rows(1)] = part_ref[PACKED:]

        @pl.when(use_a)
        def _():
            take(part_a)

        @pl.when(jnp.logical_not(use_a))
        def _():
            take(part_b)

    residual_ref[rows(0)] = right_ref[...]
    if flag == 0:
        residual_ref[rows(1)] = shared_ref[...]
    invert(factors_ref, a_ref)
    for k in range(2):
        lifted_ref[rows(k)] = fine_dot(factors_ref[k], residual_ref[rows(k)])


def begin_kernel(even_ref, from_slab, slab_b, slab_a, blocks_ref, first_ref, primal_ref, patch_residual_ref,
                 patch_lifted_ref, factors_ref, residual_ref, lifted_ref, rounded_ref, c_ref, a_ref, some_ref, solved_ref):
    invert_kernel(0, even_ref, slab_b, slab_a, blocks_ref, first_ref, from_slab, factors_ref, some_ref, solved_ref, a_ref)
    for k in range(2):
        for flag, part, solved in ((0, some_ref, solved_ref), (1, patch_residual_ref, patch_lifted_ref)):
            residual_ref[rows(2 * k + flag)] = part[rows(k)]
            lifted_ref[rows(2 * k + flag)] = solved[rows(k)]
    rounded_ref[...] = lifted_ref[...].astype(jnp.bfloat16)
    restrict(primal_ref, rounded_ref, c_ref)


def invert(out_ref, a_ref):
    index = lax.broadcasted_iota(jnp.int32, (F, F), 0)
    unit = (index == lax.broadcasted_iota(jnp.int32, (F, F), 1)).astype(jnp.float32)

    def start(f, safe):
        diagonal = jnp.sum(unit * a_ref[f], axis=0, keepdims=True)
        if not safe:
            return unit / diagonal
        ratio = jnp.sum(jnp.abs(a_ref[f]), axis=0, keepdims=True) / diagonal
        return unit * (1.9 / (jnp.max(ratio, axis=1, keepdims=True) * diagonal))

    for f in range(2):
        out_ref[f] = start(f, False)

    def newton(multiply):
        lefts = [unit - multiply(a_ref[f], out_ref[f]) for f in range(2)]
        worst = jnp.float32(0.0)
        for f in range(2):
            worst = jnp.maximum(worst, jnp.sum(lefts[f] * lefts[f]))
        for f in range(2):
            out_ref[f] = out_ref[f] + multiply(out_ref[f], lefts[f])
        return worst

    def rough(a, b):
        return rough_dot(a.astype(jnp.bfloat16), b.astype(jnp.bfloat16))

    def rough_body(carry):
        step, _ = carry
        newton(rough)
        return step + 1, newton(rough)

    lax.while_loop(lambda c: (c[0] < ROUGH_STEPS) & ~(c[1] < 0.25), rough_body, (0, jnp.float32(1e30)))

    good = newton(fine_dot) < 0.5
    worst = jnp.where(good, newton(fine_dot), 1e30)

    @pl.when(jnp.logical_not(good))
    def _():
        for f in range(2):
            out_ref[f] = start(f, True)

    def fine_body(carry):
        step, last, _ = carry
        newton(fine_dot)
        return step + 1, newton(fine_dot), last

    lax.while_loop(
        lambda c: (c[0] < FINE_STEPS) & (c[1] > 1e-6) & ~((c[1] < 1e-2) & (c[1] >= c[2])),
        fine_body, (0, worst, jnp.float32(1e31)))


def restrict(primal_ref, rounded_ref, c_ref):
    c = rough_dot(primal_ref[...], rounded_ref[...]).astype(jnp.bfloat16)
    for j in range(32):
        c_ref[j] = c


def factor(factor_refs, f):
    return factor_refs[f % 2][f // 2]


def write_parts(even_ref, terms_ref, outs):
    slab_b, patch_b, slab_a, patch_a = outs
    for even, ahead, back, a_ref, b_ref in ((even_ref[0], 0, 2, slab_a, slab_b), (even_ref[1], 1, 3, patch_a, patch_b)):
        upper, lower = terms_ref[rows(ahead)], terms_ref[rows(back)]
        b_ref[...] = jnp.where(even == 1, lower, upper)
        a_ref[...] = jnp.where(even == 1, upper, lower)


def assembled(even_ref, terms_ref, got, f):
    slab_b, patch_b, slab_a, patch_a = got
    a_ref, b_ref = ((slab_a, slab_b), (patch_a, patch_b))[f % 2]
    use_a = even_ref[f % 2] == (1 if f < 2 else 0)
    return terms_ref[rows(f)] + jnp.where(use_a, a_ref[...], b_ref[...])


def coarse_kernel(coarse_ref, gathered_ref, out_ref):
    gathered = gathered_ref[...].reshape(OWN, RHS)
    out_ref[...] = rough_dot(coarse_ref[...], gathered).reshape(16, PRIM, RHS)


def repeat_rows(out_ref, value):
    for j in range(out_ref.shape[0]):
        out_ref[j] = value


def sum_kernel(parts_ref, out_ref):
    repeat_rows(out_ref, jnp.sum(parts_ref[...], axis=0))


def terms_kernel(even_ref, parts_ref, inverse_ref, rounded_ref, primal_ref, residual_ref, lifted_ref, terms_ref,
                 product_ref, *outs):
    u = jnp.sum(parts_ref[...], axis=0).astype(jnp.bfloat16)
    product = jnp.zeros((1, RHS), jnp.float32)
    for f in range(4):
        term = rough_dot(inverse_ref[rows(f)], rounded_ref[...]) + lax.dot_general(
            primal_ref[:, rows(f)], u, (((0,), (0,)), ((), ())), preferred_element_type=jnp.float32)
        terms_ref[rows(f)] = term
        lifted = lifted_ref[rows(f)]
        weight = term + residual_ref[rows(f)] if f < 2 else term
        product = product + jnp.sum(lifted * weight, axis=0, keepdims=True)
    repeat_rows(product_ref, product)
    write_parts(even_ref, terms_ref, outs)


def direction_kernel(again, *refs):
    if again:
        sums_ref, before_ref, last_ref, *refs = refs
        scale = jnp.sum(sums_ref[...], axis=0) / jnp.sum(before_ref[...], axis=0)[:1]
    else:
        over_ref, *refs = refs
    (even_ref, terms_ref, slab_b, patch_b, slab_a, patch_a, lifted_ref, slab_factors, patch_factors, blocks_ref, inverse_ref,
     direction_ref, image_ref, product_ref, *outs, rounded_ref) = refs
    got = (slab_b, patch_b, slab_a, patch_a)
    for f in range(4):
        value = lifted_ref[rows(f)] + fine_dot(factor((slab_factors, patch_factors), f), assembled(even_ref, terms_ref, got, f))
        if again:
            value = value + scale * last_ref[rows(f)]
        direction_ref[rows(f)] = value
        rounded_ref[rows(f)] = value.astype(jnp.bfloat16)
    product = jnp.zeros((1, RHS), jnp.float32)
    for f in range(4):
        image = rough_dot(blocks_ref[f], rounded_ref[rows(f)]) - rough_dot(inverse_ref[rows(f)], rounded_ref[...])
        image_ref[rows(f)] = image
        product = product + jnp.sum(direction_ref[rows(f)] * image, axis=0, keepdims=True)
    repeat_rows(product_ref, product if again else jnp.concatenate([over_ref[0], product], axis=0))
    if again:
        outs[0][...] = image_ref[rows(2)]
        outs[1][...] = image_ref[rows(3)]
    else:
        write_parts(even_ref, image_ref, outs)


def update_kernel(even_ref, sums_ref, image_ref, slab_b, patch_b, slab_a, patch_a, last_ref, slab_factors,
                  patch_factors, primal_ref, residual_ref, lifted_ref, rounded_ref, c_ref):
    sums = jnp.sum(sums_ref[...], axis=0)
    step = sums[:1] / sums[1:]
    got = (slab_b, patch_b, slab_a, patch_a)
    for f in range(4):
        residual_ref[rows(f)] = last_ref[rows(f)] - step * assembled(even_ref, image_ref, got, f)
        lifted = fine_dot(factor((slab_factors, patch_factors), f), residual_ref[rows(f)])
        lifted_ref[rows(f)] = lifted
        rounded_ref[rows(f)] = lifted.astype(jnp.bfloat16)
    restrict(primal_ref, rounded_ref, c_ref)


def last_kernel(first_ref, over_ref, under_ref, first_direction_ref, direction_ref, residual_ref, image_ref,
                slab_ref, patch_ref, solution_ref, out_ref):
    first = jnp.sum(first_ref[...], axis=0)
    first_step = first[:1] / first[1:]
    step = jnp.sum(over_ref[...], axis=0) / jnp.sum(under_ref[...], axis=0)
    for f, got in ((0, slab_ref), (1, patch_ref)):
        value = first_step * first_direction_ref[rows(f)] + step * direction_ref[rows(f)]
        left = residual_ref[rows(f)] - step * (image_ref[rows(f)] + got[...])
        solution_ref[:, f, :] = value.T
        out_ref[:, f, :] = left.T


def swap(parts):
    slab_b, patch_b, slab_a, patch_a = parts
    return (
        lax.ppermute(slab_b, SLAB, even_pairs(32)),
        lax.ppermute(patch_b, PATCH, even_pairs(16)),
        lax.ppermute(slab_a, SLAB, odd_pairs(32)),
        lax.ppermute(patch_a, PATCH, odd_pairs(16)),
    )


def total_parts(spread):
    parts = lax.all_to_all(spread, COLUMN, 0, 0)
    spread = call(sum_kernel, f32(16, *spread.shape[1:]), [VMEM], "sum")(parts)
    return lax.all_to_all(spread, PLANE, 0, 0)


def on_device(rhs, face_blocks, interior_inverse, coarse_inverse, primal_ids):
    blocks = face_blocks[0, 0]
    inverse = interior_inverse[0, 0]
    ids = primal_ids[0, 0]
    slab_even = 1 - lax.axis_index("x") % 2
    patch_even = 1 - lax.axis_index("core")
    even = jnp.stack([slab_even, patch_even]).astype(jnp.int32)

    first, second = call(turn_kernel, [f32(F, RHS)] * 2, [VMEM], "turn")(rhs[0, 0])
    from_slab = lax.ppermute(first, SLAB, roll_pairs(32, 1))
    send = call(
        pack_kernel, [bf16(PACKED, HALF), f32(PACKED + F, HALF)] * 2, [SMEM, VMEM, VMEM], "pack")(even, second, blocks)
    got = swap(send)
    primal = call(primal_kernel, bf16(PRIM, NI), [SMEM, VMEM], "primal")(ids, blocks)
    field = f32(NI, RHS)
    part = [f32(F, RHS)] * 4
    solved = [field, field, bf16(NI, RHS), bf16(32, PRIM, RHS)]
    solve_flops = 4 * 12 * F * F * RHS

    def coarse_terms(residual, lifted, rounded, c):
        gathered = lax.all_to_all(c, SLAB, 0, 0)
        partial = call(coarse_kernel, f32(16, PRIM, RHS), [VMEM] * 2, "coarse", 1 << 25)(coarse_inverse, gathered)
        parts = lax.all_to_all(partial, PATCH, 0, 0)
        terms, product, *send = call(
            terms_kernel, [field, f32(32, 1, RHS)] + part, [SMEM] + [VMEM] * 6, "terms", 1 << 28)(
                even, parts, inverse, rounded, primal, residual, lifted)
        return terms, product, send

    scratch = [pltpu.VMEM((NI, RHS), jnp.bfloat16)]
    pair = [f32(2, F, F), f32(2 * F, RHS), f32(2 * F, RHS)]
    square = pltpu.VMEM((2, F, F), jnp.float32)
    patch_factors, patch_residual, patch_lifted = call(
        lambda even_ref, part_b, part_a, blocks_ref, right_ref, *refs: invert_kernel(
            1, even_ref, part_b, part_a, blocks_ref, right_ref, None, *refs),
        pair, [SMEM] + [VMEM] * 4, "invert", 1 << 32, [square])(even, got[1], got[3], blocks, second)
    slab_factors, residual, lifted, rounded, c = call(
        begin_kernel, pair[:1] + solved, [SMEM] + [VMEM] * 8, "begin", 1 << 32,
        [square, pltpu.VMEM((2 * F, RHS), jnp.float32), pltpu.VMEM((2 * F, RHS), jnp.float32)])(
            even, from_slab, got[0], got[2], blocks, first, primal, patch_residual, patch_lifted)
    factors = (slab_factors, patch_factors)
    terms, product, send = coarse_terms(residual, lifted, rounded, c)
    got = swap(send)
    first_direction, image, spread, *send = call(
        lambda *refs: direction_kernel(False, *refs), [field, field, f32(32, 2, RHS)] + part,
        [VMEM, SMEM] + [VMEM] * 10, "direction", solve_flops, scratch)(
            product, even, terms, *got, lifted, *factors, blocks, inverse)

    got = swap(send)
    first_sums = total_parts(spread)
    residual, lifted, rounded, c = call(update_kernel, solved, [SMEM] + [VMEM] * 10, "update", solve_flops)(
        even, first_sums, image, *got, residual, *factors, primal)
    terms, spread, send = coarse_terms(residual, lifted, rounded, c)
    got = swap(send)
    over = total_parts(spread)
    direction, image, spread, *send = call(
        lambda *refs: direction_kernel(True, *refs), [field, field, f32(32, 1, RHS)] + part[:2],
        [VMEM] * 3 + [SMEM] + [VMEM] * 10, "direction_again", solve_flops, scratch)(
            over, first_sums, first_direction, even, terms, *got, lifted, *factors, blocks, inverse)

    from_slab = lax.ppermute(send[0], SLAB, roll_pairs(32, -1))
    from_patch = lax.ppermute(send[1], PATCH, roll_pairs(16, -1))
    under = total_parts(spread)
    solution, residual = call(last_kernel, [f32(RHS, 2, F)] * 2, [VMEM] * 9, "last")(
        first_sums, over, under, first_direction, direction, residual, image, from_slab, from_patch)
    return (solution.reshape(1, 1, RHS, 2, F), residual.reshape(1, 1, RHS, 2, F))


def solution(mesh):
    chips = Mesh(mesh.devices.reshape(2, 4, 4, 8, 2), ("zh", "y", "x", "zl", "core"))
    return jax.shard_map(
        on_device,
        mesh=chips,
        in_specs=(
            P(SLAB, PATCH, None, None, None),
            P(SLAB, PATCH, None, None, None),
            P(SLAB, PATCH, None, None),
            P(SLAB, PATCH),
            P(SLAB, PATCH, None),
        ),
        out_specs=(P(SLAB, PATCH, None, None, None), P(SLAB, PATCH, None, None, None)),
        check_vma=False,
    )
```

```python
import jax
import jax.numpy as jnp
from jax import lax
from jax.experimental import pallas as pl
from jax.experimental.pallas import tpu as pltpu
from jax.sharding import Mesh, PartitionSpec as P

F = 256
NI = 1024
RHS = 128
PRIM = 16
OWN = 2 * F
SLAB = ("zh", "y", "x")
PATCH = ("zl", "core")
COLUMN = ("zh", "zl", "core")
PLANE = ("y", "x")
HIGHEST = lax.Precision.HIGHEST
ROUGH_STEPS = 6
FINE_STEPS = 32
VMEM = pl.BlockSpec(memory_space=pltpu.VMEM)
SMEM = pl.BlockSpec(memory_space=pltpu.SMEM)


def odd_pairs(count):
    return [(i, i ^ 1) for i in range(count)]


def even_pairs(count):
    return [(i, (i + 1) % count if i % 2 else (i - 1) % count) for i in range(count)]


def roll_pairs(count, by):
    return [(i, (i + by) % count) for i in range(count)]


def call(kernel, out_shapes, in_specs, name, flops=0, scratch=()):
    return pl.pallas_call(
        kernel,
        out_shape=out_shapes,
        in_specs=in_specs,
        out_specs=jax.tree.map(lambda _: VMEM, out_shapes),
        scratch_shapes=list(scratch),
        compiler_params=pltpu.CompilerParams(vmem_limit_bytes=16 * 1024 * 1024),
        cost_estimate=pl.CostEstimate(flops=flops, bytes_accessed=1 << 20, transcendentals=0),
        name=name,
    )


def f32(*shape):
    return jax.ShapeDtypeStruct(shape, jnp.float32)


def bf16(*shape):
    return jax.ShapeDtypeStruct(shape, jnp.bfloat16)


def fine_dot(a, b):
    return jnp.dot(a, b, precision=HIGHEST, preferred_element_type=jnp.float32)


def rough_dot(a, b):
    return jnp.dot(a, b, preferred_element_type=jnp.float32)


def rows(number):
    return slice(number * F, (number + 1) * F)


HALF = F // 2
PAD = 16
PACKED = F + PAD


def square_masks():
    row = lax.broadcasted_iota(jnp.int32, (HALF, HALF), 0)
    column = lax.broadcasted_iota(jnp.int32, (HALF, HALF), 1)
    return row > column, row == column, row < column


def turn_kernel(rhs_ref, first_ref, second_ref):
    first_ref[...] = rhs_ref[:, 0, :].T
    second_ref[...] = rhs_ref[:, 1, :].T


def pack_kernel(even_ref, second_ref, blocks_ref, slab_b, patch_b, slab_a, patch_a):
    lower, diagonal, upper = square_masks()
    for f in range(4):
        b_ref, a_ref = ((slab_b, slab_a), (patch_b, patch_a))[f % 2]
        use_a = even_ref[f % 2] == (1 if f < 2 else 0)

        def pack(out_ref):
            kind = out_ref.dtype
            block = blocks_ref[f].astype(jnp.float32)
            first, second = block[:HALF, :HALF], block[HALF:, HALF:]
            out_ref[:HALF] = jnp.where(upper, second, first).astype(kind)
            out_ref[HALF:F] = block[HALF:, :HALF].astype(kind)
            row = jnp.sum(jnp.where(diagonal, second, 0.0), axis=0, keepdims=True)
            out_ref[F:PACKED] = jnp.broadcast_to(row, (PAD, HALF)).astype(kind)
            if f % 2:
                out_ref[PACKED:] = second_ref[...]

        @pl.when(use_a)
        def _():
            pack(a_ref)

        @pl.when(jnp.logical_not(use_a))
        def _():
            pack(b_ref)


def unpack(part_ref, out_ref):
    lower, diagonal, upper = square_masks()
    mixed, below = part_ref[:HALF].astype(jnp.float32), part_ref[HALF:F].astype(jnp.float32)
    corner = part_ref[F:PACKED].astype(jnp.float32)[:1]
    first = jnp.where(upper, 0.0, mixed)
    second = jnp.where(upper, mixed, 0.0)
    out_ref[:HALF, :HALF] = out_ref[:HALF, :HALF] + (first + jnp.where(lower, first, 0.0).T)
    out_ref[HALF:, HALF:] = out_ref[HALF:, HALF:] + (
        second + second.T + jnp.where(diagonal, corner, 0.0))
    out_ref[HALF:, :HALF] = out_ref[HALF:, :HALF] + below
    out_ref[:HALF, HALF:] = out_ref[:HALF, HALF:] + below.T


def primal_kernel(even_ref, ids_ref, blocks_ref, coarse_ref, after_ref, primal_ref, sent_ref):
    sent_ref[...] = jnp.where(even_ref[2] == 1, coarse_ref[:, :F], coarse_ref[:, F:])
    row = lax.broadcasted_iota(jnp.int32, (PRIM, NI), 0)
    picked = jnp.zeros((PRIM, NI), jnp.int32)
    for k in range(PRIM):
        picked = jnp.where(row == k, ids_ref[k], picked)
    onehot = (picked == lax.broadcasted_iota(jnp.int32, (PRIM, NI), 1)).astype(jnp.float32).astype(jnp.bfloat16)
    for f in range(4):
        primal_ref[:, rows(f)] = rough_dot(onehot[:, rows(f)], blocks_ref[f]).astype(jnp.bfloat16)


def invert_kernel(flag, even_ref, part_b, part_a, blocks_ref, right_ref, shared_ref, factors_ref, residual_ref,
                  lifted_ref, a_ref):
    for k in range(2):
        use_a = even_ref[flag] == 1 - k
        a_ref[k] = blocks_ref[2 * k + flag].astype(jnp.float32)

        def take(part_ref):
            unpack(part_ref, a_ref.at[k])
            if k == 1 and flag == 1:
                residual_ref[rows(1)] = part_ref[PACKED:]

        @pl.when(use_a)
        def _():
            take(part_a)

        @pl.when(jnp.logical_not(use_a))
        def _():
            take(part_b)

    residual_ref[rows(0)] = right_ref[...]
    if flag == 0:
        residual_ref[rows(1)] = shared_ref[...]
    invert(factors_ref, a_ref)
    for k in range(2):
        lifted_ref[rows(k)] = fine_dot(factors_ref[k], residual_ref[rows(k)])


def begin_kernel(even_ref, from_slab, slab_b, slab_a, blocks_ref, first_ref, patch_residual_ref,
                 patch_lifted_ref, factors_ref, residual_ref, lifted_ref, rounded_ref, a_ref, some_ref, solved_ref):
    invert_kernel(0, even_ref, slab_b, slab_a, blocks_ref, first_ref, from_slab, factors_ref, some_ref, solved_ref, a_ref)
    for k in range(2):
        for flag, part, solved in ((0, some_ref, solved_ref), (1, patch_residual_ref, patch_lifted_ref)):
            residual_ref[rows(2 * k + flag)] = part[rows(k)]
            lifted_ref[rows(2 * k + flag)] = solved[rows(k)]
    rounded_ref[...] = lifted_ref[...].astype(jnp.bfloat16)


def merge_kernel(even_ref, kept_ref, swapped_ref, primal_ref, rounded_ref, c_ref, coarse_ref):
    high = even_ref[2] == 1
    kept = jnp.where(high, kept_ref[:, F:], kept_ref[:, :F])
    coarse_ref[:F] = jnp.where(high, swapped_ref[...], kept)
    coarse_ref[F:] = jnp.where(high, kept, swapped_ref[...])
    restrict(primal_ref, rounded_ref, c_ref)


def invert(out_ref, a_ref):
    index = lax.broadcasted_iota(jnp.int32, (F, F), 0)
    unit = (index == lax.broadcasted_iota(jnp.int32, (F, F), 1)).astype(jnp.float32)

    def start(f, safe):
        diagonal = jnp.sum(unit * a_ref[f], axis=0, keepdims=True)
        if not safe:
            return unit / diagonal
        ratio = jnp.sum(jnp.abs(a_ref[f]), axis=0, keepdims=True) / diagonal
        return unit * (1.9 / (jnp.max(ratio, axis=1, keepdims=True) * diagonal))

    for f in range(2):
        out_ref[f] = start(f, False)

    def newton(multiply):
        lefts = [unit - multiply(a_ref[f], out_ref[f]) for f in range(2)]
        worst = jnp.float32(0.0)
        for f in range(2):
            worst = jnp.maximum(worst, jnp.sum(lefts[f] * lefts[f]))
        for f in range(2):
            out_ref[f] = out_ref[f] + multiply(out_ref[f], lefts[f])
        return worst

    def rough(a, b):
        return rough_dot(a.astype(jnp.bfloat16), b.astype(jnp.bfloat16))

    def rough_body(carry):
        step, _ = carry
        newton(rough)
        return step + 1, newton(rough)

    lax.while_loop(lambda c: (c[0] < ROUGH_STEPS) & ~(c[1] < 0.25), rough_body, (0, jnp.float32(1e30)))

    good = newton(fine_dot) < 0.5
    worst = jnp.where(good, newton(fine_dot), 1e30)

    @pl.when(jnp.logical_not(good))
    def _():
        for f in range(2):
            out_ref[f] = start(f, True)

    def fine_body(carry):
        step, last, _ = carry
        newton(fine_dot)
        return step + 1, newton(fine_dot), last

    lax.while_loop(
        lambda c: (c[0] < FINE_STEPS) & (c[1] > 1e-6) & ~((c[1] < 1e-2) & (c[1] >= c[2])),
        fine_body, (0, worst, jnp.float32(1e31)))


def restrict(primal_ref, rounded_ref, c_ref):
    c = rough_dot(primal_ref[...], rounded_ref[...]).astype(jnp.bfloat16)
    for j in range(32):
        c_ref[j] = c


def factor(factor_refs, f):
    return factor_refs[f % 2][f // 2]


def write_parts(even_ref, terms_ref, outs):
    slab_b, patch_b, slab_a, patch_a = outs
    for even, ahead, back, a_ref, b_ref in ((even_ref[0], 0, 2, slab_a, slab_b), (even_ref[1], 1, 3, patch_a, patch_b)):
        upper, lower = terms_ref[rows(ahead)], terms_ref[rows(back)]
        b_ref[...] = jnp.where(even == 1, lower, upper)
        a_ref[...] = jnp.where(even == 1, upper, lower)


def assembled(even_ref, terms_ref, got, f):
    slab_b, patch_b, slab_a, patch_a = got
    a_ref, b_ref = ((slab_a, slab_b), (patch_a, patch_b))[f % 2]
    use_a = even_ref[f % 2] == (1 if f < 2 else 0)
    return terms_ref[rows(f)] + jnp.where(use_a, a_ref[...], b_ref[...])


def coarse_kernel(coarse_ref, gathered_ref, out_ref):
    gathered = gathered_ref[...].reshape(2 * F, RHS)
    out_ref[...] = lax.dot_general(
        coarse_ref[...], gathered, (((0,), (0,)), ((), ())), preferred_element_type=jnp.float32
    ).reshape(16, PRIM, RHS)


def repeat_rows(out_ref, value):
    for j in range(out_ref.shape[0]):
        out_ref[j] = value


def sum_kernel(parts_ref, out_ref):
    repeat_rows(out_ref, jnp.sum(parts_ref[...], axis=0))


def terms_kernel(even_ref, parts_ref, inverse_ref, rounded_ref, primal_ref, residual_ref, lifted_ref, terms_ref,
                 product_ref, *outs):
    u = jnp.sum(parts_ref[...], axis=0).astype(jnp.bfloat16)
    product = jnp.zeros((1, RHS), jnp.float32)
    for f in range(4):
        term = rough_dot(inverse_ref[rows(f)], rounded_ref[...]) + lax.dot_general(
            primal_ref[:, rows(f)], u, (((0,), (0,)), ((), ())), preferred_element_type=jnp.float32)
        terms_ref[rows(f)] = term
        lifted = lifted_ref[rows(f)]
        weight = term + residual_ref[rows(f)] if f < 2 else term
        product = product + jnp.sum(lifted * weight, axis=0, keepdims=True)
    repeat_rows(product_ref, product)
    write_parts(even_ref, terms_ref, outs)


def direction_kernel(again, *refs):
    if again:
        sums_ref, before_ref, last_ref, *refs = refs
        scale = jnp.sum(sums_ref[...], axis=0) / jnp.sum(before_ref[...], axis=0)[:1]
    else:
        over_ref, *refs = refs
    (even_ref, terms_ref, slab_b, patch_b, slab_a, patch_a, lifted_ref, slab_factors, patch_factors, blocks_ref, inverse_ref,
     direction_ref, image_ref, product_ref, *outs, rounded_ref) = refs
    got = (slab_b, patch_b, slab_a, patch_a)
    for f in range(4):
        value = lifted_ref[rows(f)] + fine_dot(factor((slab_factors, patch_factors), f), assembled(even_ref, terms_ref, got, f))
        if again:
            value = value + scale * last_ref[rows(f)]
        direction_ref[rows(f)] = value
        rounded_ref[rows(f)] = value.astype(jnp.bfloat16)
    product = jnp.zeros((1, RHS), jnp.float32)
    for f in range(4):
        image = rough_dot(blocks_ref[f], rounded_ref[rows(f)]) - rough_dot(inverse_ref[rows(f)], rounded_ref[...])
        image_ref[rows(f)] = image
        product = product + jnp.sum(direction_ref[rows(f)] * image, axis=0, keepdims=True)
    repeat_rows(product_ref, product if again else jnp.concatenate([over_ref[0], product], axis=0))
    if again:
        outs[0][...] = image_ref[rows(2)]
        outs[1][...] = image_ref[rows(3)]
    else:
        write_parts(even_ref, image_ref, outs)


def update_kernel(even_ref, sums_ref, image_ref, slab_b, patch_b, slab_a, patch_a, last_ref, slab_factors,
                  patch_factors, primal_ref, residual_ref, lifted_ref, rounded_ref, c_ref):
    sums = jnp.sum(sums_ref[...], axis=0)
    step = sums[:1] / sums[1:]
    got = (slab_b, patch_b, slab_a, patch_a)
    for f in range(4):
        residual_ref[rows(f)] = last_ref[rows(f)] - step * assembled(even_ref, image_ref, got, f)
        lifted = fine_dot(factor((slab_factors, patch_factors), f), residual_ref[rows(f)])
        lifted_ref[rows(f)] = lifted
        rounded_ref[rows(f)] = lifted.astype(jnp.bfloat16)
    restrict(primal_ref, rounded_ref, c_ref)


def last_kernel(first_ref, over_ref, under_ref, first_direction_ref, direction_ref, residual_ref, image_ref,
                slab_ref, patch_ref, solution_ref, out_ref):
    first = jnp.sum(first_ref[...], axis=0)
    first_step = first[:1] / first[1:]
    step = jnp.sum(over_ref[...], axis=0) / jnp.sum(under_ref[...], axis=0)
    for f, got in ((0, slab_ref), (1, patch_ref)):
        value = first_step * first_direction_ref[rows(f)] + step * direction_ref[rows(f)]
        left = residual_ref[rows(f)] - step * (image_ref[rows(f)] + got[...])
        solution_ref[:, f, :] = value.T
        out_ref[:, f, :] = left.T


def swap(parts):
    slab_b, patch_b, slab_a, patch_a = parts
    return (
        lax.ppermute(slab_b, SLAB, even_pairs(32)),
        lax.ppermute(patch_b, PATCH, even_pairs(16)),
        lax.ppermute(slab_a, SLAB, odd_pairs(32)),
        lax.ppermute(patch_a, PATCH, odd_pairs(16)),
    )


def total_parts(spread):
    parts = lax.all_to_all(spread, COLUMN, 0, 0)
    spread = call(sum_kernel, f32(16, *spread.shape[1:]), [VMEM], "sum")(parts)
    return lax.all_to_all(spread, PLANE, 0, 0)


def on_device(rhs, face_blocks, interior_inverse, coarse_inverse, primal_ids):
    blocks = face_blocks[0, 0]
    inverse = interior_inverse[0, 0]
    ids = primal_ids[0, 0]
    slab_even = 1 - lax.axis_index("x") % 2
    patch_even = 1 - lax.axis_index("core")
    even = jnp.stack([slab_even, patch_even, lax.axis_index("zh")]).astype(jnp.int32)

    first, second = call(turn_kernel, [f32(F, RHS)] * 2, [VMEM], "turn")(rhs[0, 0])
    from_slab = lax.ppermute(first, SLAB, roll_pairs(32, 1))
    send = call(
        pack_kernel, [bf16(PACKED, HALF), f32(PACKED + F, HALF)] * 2, [SMEM, VMEM, VMEM], "pack")(even, second, blocks)
    got = swap(send)
    primal, *sent = call(primal_kernel, [bf16(PRIM, NI), bf16(F, F)], [SMEM, SMEM, VMEM, VMEM, pl.BlockSpec(memory_space=pl.ANY)], "primal")(
        even, ids, blocks, coarse_inverse, got[3])
    swapped = lax.ppermute(sent[0], "zh", [(0, 1), (1, 0)])
    field = f32(NI, RHS)
    part = [f32(F, RHS)] * 4
    solved = [field, field, bf16(NI, RHS), bf16(32, PRIM, RHS)]
    solve_flops = 4 * 12 * F * F * RHS

    def coarse_terms(residual, lifted, rounded, c):
        gathered = lax.all_to_all(c, COLUMN, 0, 0)
        partial = call(coarse_kernel, f32(16, PRIM, RHS), [VMEM] * 2, "coarse", 1 << 25)(coarse, gathered)
        parts = lax.all_to_all(partial, PLANE, 0, 0)
        terms, product, *send = call(
            terms_kernel, [field, f32(32, 1, RHS)] + part, [SMEM] + [VMEM] * 6, "terms", 1 << 28)(
                even, parts, inverse, rounded, primal, residual, lifted)
        return terms, product, send

    scratch = [pltpu.VMEM((NI, RHS), jnp.bfloat16)]
    pair = [f32(2, F, F), f32(2 * F, RHS), f32(2 * F, RHS)]
    square = pltpu.VMEM((2, F, F), jnp.float32)
    patch_factors, patch_residual, patch_lifted = call(
        lambda even_ref, part_b, part_a, blocks_ref, right_ref, *refs: invert_kernel(
            1, even_ref, part_b, part_a, blocks_ref, right_ref, None, *refs),
        pair, [SMEM] + [VMEM] * 4, "invert", 1 << 32, [square])(even, got[1], got[3], blocks, second)
    slab_factors, residual, lifted, rounded = call(
        begin_kernel, pair[:1] + solved[:3], [SMEM] + [VMEM] * 7, "begin", 0,
        [square, pltpu.VMEM((2 * F, RHS), jnp.float32), pltpu.VMEM((2 * F, RHS), jnp.float32)])(
            even, from_slab, got[0], got[2], blocks, first, patch_residual, patch_lifted)
    c, coarse = call(merge_kernel, [solved[3], bf16(2 * F, F)], [SMEM] + [VMEM] * 4, "merge")(
        even, coarse_inverse, swapped, primal, rounded)
    factors = (slab_factors, patch_factors)
    terms, product, send = coarse_terms(residual, lifted, rounded, c)
    got = swap(send)
    first_direction, image, spread, *send = call(
        lambda *refs: direction_kernel(False, *refs), [field, field, f32(32, 2, RHS)] + part,
        [VMEM, SMEM] + [VMEM] * 10, "direction", solve_flops, scratch)(
            product, even, terms, *got, lifted, *factors, blocks, inverse)

    got = swap(send)
    first_sums = total_parts(spread)
    residual, lifted, rounded, c = call(update_kernel, solved, [SMEM] + [VMEM] * 10, "update", solve_flops)(
        even, first_sums, image, *got, residual, *factors, primal)
    terms, spread, send = coarse_terms(residual, lifted, rounded, c)
    got = swap(send)
    over = total_parts(spread)
    direction, image, spread, *send = call(
        lambda *refs: direction_kernel(True, *refs), [field, field, f32(32, 1, RHS)] + part[:2],
        [VMEM] * 3 + [SMEM] + [VMEM] * 10, "direction_again", solve_flops, scratch)(
            over, first_sums, first_direction, even, terms, *got, lifted, *factors, blocks, inverse)

    from_slab = lax.ppermute(send[0], SLAB, roll_pairs(32, -1))
    from_patch = lax.ppermute(send[1], PATCH, roll_pairs(16, -1))
    under = total_parts(spread)
    solution, residual = call(last_kernel, [f32(RHS, 2, F)] * 2, [VMEM] * 9, "last")(
        first_sums, over, under, first_direction, direction, residual, image, from_slab, from_patch)
    return (solution.reshape(1, 1, RHS, 2, F), residual.reshape(1, 1, RHS, 2, F))


def solution(mesh):
    chips = Mesh(mesh.devices.reshape(2, 4, 4, 8, 2), ("zh", "y", "x", "zl", "core"))
    return jax.shard_map(
        on_device,
        mesh=chips,
        in_specs=(
            P(SLAB, PATCH, None, None, None),
            P(SLAB, PATCH, None, None, None),
            P(SLAB, PATCH, None, None),
            P(SLAB, PATCH),
            P(SLAB, PATCH, None),
        ),
        out_specs=(P(SLAB, PATCH, None, None, None), P(SLAB, PATCH, None, None, None)),
        check_vma=False,
    )
```
